1024 devices in a mesh: dp: 64 (over z_lo, y, core), mp: 16 (over x, z_hi).
Axes of the slice: x: 4, y: 4, z: 32 (z_hi: 4, z_lo: 8; z = z_hi * 8 + z_lo), core: 2. Of those that a mesh axis runs over, the one named last changes fastest.
Arguments:
- attn_out: bfloat16 [16384, 3072], P('dp', 'mp'), may hold values from -6 to 6
- w_out: bfloat16 [3072, 3072], P('mp', 'dp'), may hold values from -0.109375 to 0.109375
- cotangent: bfloat16 [16384, 3072], P('dp', 'mp'), may hold values from -16 to 16
Outputs:
- projected: bfloat16 [16384, 3072], P('dp', 'mp')
- attn_grad: bfloat16 [16384, 3072], P('dp', 'mp')
- weight_grad: float32 [3072, 3072], P('mp', 'dp')
The draws below stay inside these ranges and needn't reach their ends.
All inputs are finite; a program needn't handle non-finite values.
Results may differ from the reference program's by a relative error of at most 0.018.
Values may be sent and summed in bfloat16 or wider, within the bound.
A program may use at most 32 MiB of HBM per device.

```python
import jax
import jax.numpy as jnp
from jax import lax

K = 3072
DW = 3072
TOKENS = 16384
N_MP = 16


def raised(result, rng, source, target, shards_of, factor):
    def block_of(axis_at):
        return (jnp.arange(result.shape[axis_at]) // (result.shape[axis_at] // shards_of)).reshape((-1,) + (1,) * (result.ndim - 1 - axis_at))

    one_side = jax.random.permutation(rng, shards_of)[block_of(target)]
    far = (block_of(target) + shards_of // 2) % shards_of
    return jnp.where((block_of(source) == one_side) | (block_of(source) == far), factor * result, result)


def steps_of(key, shape, pieces, smallest, top_value):
    loudness, own = 1.0, jax.random.fold_in(key, 6)
    for axis_at, parts in pieces:
        draws = jnp.exp(jax.random.uniform(jax.random.fold_in(own, axis_at), (parts,), jnp.float32, smallest / len(pieces), top_value / len(pieces)))
        loudness = loudness * jnp.repeat(draws, shape[axis_at] // parts).reshape([-1 if axis == axis_at else 1 for axis in range(len(shape))])
    return loudness


def gaussian(own_key, dims, width, limit, split=(), kind=jnp.bfloat16):
    array = jax.random.normal(own_key, dims, jnp.float32) * width
    if len(split) > 0:
        array = steps_of(own_key, dims, split, -0.22, 0.18) * array
    return jnp.clip(array, min=-limit, max=limit).astype(kind)


def gaussian_with(stream_key, dims, width, limit, cuts, heavy, held_as=jnp.bfloat16):
    array = width * jax.random.normal(stream_key, dims, jnp.float32)
    if cuts:
        array = array * steps_of(stream_key, dims, cuts, -0.22, 0.18)
    return jnp.clip(raised(array, jax.random.fold_in(stream_key, 3), *heavy), -limit, limit).astype(held_as)


def setup_inputs(seed: int = 0) -> dict:
    key_of = jax.random.split(jax.random.key(seed), 4)
    attn_out = gaussian(key_of[0], (TOKENS, K), 1.0, 6.0, ((0, 64), (1, 16)))
    w_out = gaussian(key_of[1], (K, DW), K ** -0.5, 0.109375, ((0, 16), (1, 64)))
    cotangent = gaussian_with(key_of[2], (TOKENS, DW), 1.0, 16.0, ((0, 64), (1, 16)), (0, 1, 64, 4.0))
    return {"attn_out": attn_out, "w_out": w_out, "cotangent": cotangent}


def reference(attn_out, w_out, cotangent):
    block_width = K // N_MP
    total = jnp.zeros((attn_out.shape[0], w_out.shape[1]), jnp.float32)
    for block in range(N_MP):
        lower = block * block_width
        block_sum = jnp.dot(attn_out[:, lower:lower + block_width], w_out[lower:lower + block_width, :], preferred_element_type=jnp.float32)
        rounded = lax.optimization_barrier(block_sum.astype(jnp.bfloat16))
        total = total + rounded.astype(jnp.float32)
    projected = total.astype(jnp.bfloat16)
    attn_grad = jnp.dot(cotangent, w_out.T, preferred_element_type=jnp.float32).astype(jnp.bfloat16)
    weight_grad = jnp.dot(attn_out.T, cotangent, preferred_element_type=jnp.float32)
    return projected, attn_grad, weight_grad
```

```python
import functools

import jax
import jax.numpy as jnp
from jax import lax
from jax.experimental import pallas as pl
from jax.experimental.pallas import tpu as pltpu
from jax.sharding import PartitionSpec as P

BF16 = jnp.bfloat16
F32 = jnp.float32
CHUNKS = 2
LANES = 128
BLOCK = 192
SHARD = 48


def flip1(a):
    return a + 1 - 2 * (a % 2)


def flip2(a):
    return a + 2 - 4 * ((a // 2) % 2)


def flip4(a):
    return a + 4 - 8 * ((a // 4) % 2)


class Wire:
    def __init__(self, sems, index, src, dst, device):
        self.copy = pltpu.make_async_remote_copy(
            src_ref=src,
            dst_ref=dst,
            send_sem=sems[0].at[index],
            recv_sem=sems[1].at[index],
            device_id=device,
            device_id_type=pl.DeviceIdType.MESH,
        )

    def start(self):
        self.copy.start()
        return self

    def got(self):
        self.copy.wait_recv()

    def sent(self):
        self.copy.wait_send()


N_WIRES = 96


def kernel(
    x_ref, w_ref, g_ref,
    proj_ref, agrad_ref, wgrad_ref,
    xt, ct, wbuf, wown, wgot, wn,
    fpart, fgot, fsend, fzgot,
    bsend, bzgot, bown,
    gbuf, ggot, hbuf, hgot, ibuf, igot3, igot2, igot1, asend, agot,
    send_sem, recv_sem,
):
    sems = (send_sem, recv_sem)
    counter = [0]
    dp = lax.axis_index("dp")
    mp = lax.axis_index("mp")
    x, zh = mp // 4, mp % 4
    zl, y, core = dp // 8, (dp // 2) % 4, dp % 2

    def device(x=x, zh=zh, zl=zl, y=y, core=core):
        return ((zl * 4 + y) * 2 + core, x * 4 + zh)

    def wire(src, dst, to):
        counter[0] += 1
        return Wire(sems, counter[0] - 1, src, dst, to)

    near = device(zh=flip1(zh))
    far = device(zh=3 - zh)
    other = device(core=1 - core)
    x_to = [(x + d) % 4 for d in range(4)]
    y_to = [(y + d) % 4 for d in range(4)]
    l1, l2, l4 = device(zl=flip1(zl)), device(zl=flip2(zl)), device(zl=flip4(zl))

    barrier = pltpu.get_barrier_semaphore()
    partners = [near, far, other, l1, l2, l4]
    partners += [device(x=x_to[d]) for d in (1, 2, 3)]
    partners += [device(y=y_to[d]) for d in (1, 2, 3)]
    for partner in partners:
        pl.semaphore_signal(
            barrier, inc=1, device_id=partner, device_id_type=pl.DeviceIdType.MESH
        )

    za, zb = zh // 2, zh % 2

    def place(yy):
        return (yy // 2 + zb) % 2, yy % 2

    sel, half = place(y)
    keeps = (zl % 2) == ((za + sel) % 2)
    gives = (zl % 2) != ((za + sel) % 2)
    k = zl // 2

    xt_all = x_ref[...].T
    ct_all = g_ref[...].T
    for c in range(CHUNKS):
        xt[c, 0] = xt_all[:, c * LANES:(c + 1) * LANES]
        ct[c, x, 0] = ct_all[:, c * LANES:(c + 1) * LANES]
    wown[...] = w_ref[...].T

    pl.semaphore_wait(barrier, len(partners))

    w_a = wire(wown, wgot, near)

    @pl.when(gives)
    def _():
        w_a.start()

    zx = [wire(xt.at[c, 0], xt.at[c, 1], near).start() for c in range(CHUNKS)]
    zc = [wire(ct.at[c, x, 0], ct.at[c, x, 1], far).start() for c in range(CHUNKS)]
    xc0 = [
        [wire(ct.at[c, x, 0], ct.at[c, x, 0], device(x=x_to[d])).start() for d in (1, 2, 3)]
        for c in range(CHUNKS)
    ]
    xc1 = [
        [wire(ct.at[c, x, 1], ct.at[c, x, 1], device(x=x_to[d])) for d in (1, 2, 3)]
        for c in range(CHUNKS)
    ]

    def segment(kk):
        return wbuf.at[kk, sel, half, core]

    column = wbuf.at[:, sel, half, core]
    w_b1 = wire(segment(k), segment(k), l4)
    w_b2 = [wire(segment(kk), segment(kk), l2) for kk in (k, flip2(k))]
    w_b3 = wire(column, column, l1)
    w_c = [wire(column, column, device(y=y_to[d])) for d in (1, 2, 3)]

    @pl.when(keeps)
    def _():
        w_a.got()
        wbuf[k, sel, half, core] = jnp.concatenate([wown[...], wgot[...]], axis=1)
        w_b1.start()
        w_b1.got()
        for w in w_b2:
            w.start()
        for w in w_b2:
            w.got()
        w_b3.start()

    @pl.when(gives)
    def _():
        w_b3.got()

    for w in w_c:
        w.start()

    for c in range(CHUNKS):
        zc[c].got()
        for w in xc1[c]:
            w.start()

    w_d = []
    for d in range(4):
        if d:
            w_c[d - 1].got()
        s, h = place((y + 4 - d) % 4)
        part = wbuf.at[:, s, h, core]
        w_d.append(wire(part, part, other).start())
    for w in w_d:
        w.got()

    rows = 2 * BLOCK
    for kk in range(4):
        wn[:, kk * rows:(kk + 1) * rows] = wbuf[kk].reshape(rows, rows).T

    f_x, f_z, b_z = [], [], []
    for c in range(CHUNKS):
        zx[c].got()
        xval = xt[c].reshape(rows, LANES)
        for kk in range(4):
            part = jnp.dot(wbuf[kk].reshape(rows, rows), xval, preferred_element_type=F32)
            fpart[c, kk] = part.astype(BF16).reshape(2, BLOCK, LANES)
        f_x.append([
            wire(fpart.at[c, x_to[d]], fgot.at[c, d - 1], device(x=x_to[d])).start()
            for d in (1, 2, 3)
        ])
    for c in range(CHUNKS):
        for w in xc0[c] + xc1[c]:
            w.got()
        part = jnp.dot(wn[...], ct[c].reshape(4 * rows, LANES), preferred_element_type=F32)
        bown[c] = part[:BLOCK]
        bsend[c] = part[BLOCK:].astype(BF16)
        b_z.append(wire(bsend.at[c], bzgot.at[c], near).start())
        for w in f_x[c]:
            w.got()
        total = fpart[c, x].astype(F32)
        for d in range(3):
            total += fgot[c, d].astype(F32)
        fsend[c] = total[1].astype(BF16)
        f_z.append(wire(fsend.at[c], fzgot.at[c], far).start())
        fpart[c, x, 0] = total[0].astype(BF16)

    g_d = []
    for kk in range(4):
        part = jnp.zeros((rows, rows), F32)
        for c in range(CHUNKS):
            part += lax.dot_general(
                ct[c, kk].reshape(rows, LANES), xt[c].reshape(rows, LANES),
                (((1,), (1,)), ((), ())), preferred_element_type=F32,
            )
        gbuf[kk] = part.astype(BF16).reshape(2, 2, 2, SHARD, rows)
        g_d.append(wire(gbuf.at[kk, :, :, 1 - core], ggot.at[kk], other).start())
    for kk in range(4):
        g_d[kk].got()
        hbuf[:, :, kk] = (gbuf[kk, :, :, core].astype(F32) + ggot[kk].astype(F32)).astype(BF16)
    g_c = []
    for d in (1, 2, 3):
        s, h = place(y_to[d])
        g_c.append(wire(hbuf.at[s, h], hgot.at[d - 1], device(y=y_to[d])).start())
    for w in g_c:
        w.got()
    total = hbuf[sel, half].astype(F32)
    for d in range(3):
        total += hgot[d].astype(F32)
    ibuf[...] = total.astype(BF16)
    g_b3 = wire(ibuf, igot3, l1)
    g_b2 = [wire(ibuf.at[kk], igot2.at[i], l2) for i, kk in enumerate((flip1(k), 3 - k))]
    g_b1 = wire(ibuf.at[flip2(k)], igot1, l4)
    g_a = wire(asend, agot, near)

    @pl.when(gives)
    def _():
        g_b3.start()
        g_a.got()
        wgrad_ref[...] = agot[...].astype(F32)

    @pl.when(keeps)
    def _():
        g_b3.got()
        ibuf[...] = (ibuf[...].astype(F32) + igot3[...].astype(F32)).astype(BF16)
        for w in g_b2:
            w.start()
        for w in g_b2:
            w.got()
        for i, kk in enumerate((k, flip2(k))):
            ibuf[kk] = (ibuf[kk].astype(F32) + igot2[i].astype(F32)).astype(BF16)
        g_b1.start()
        g_b1.got()
        done = ibuf[k].astype(F32) + igot1[...].astype(F32)
        asend[...] = done[:, BLOCK:].astype(BF16)
        g_a.start()
        wgrad_ref[...] = done[:, :BLOCK]

    for c in range(CHUNKS):
        f_z[c].got()
        b_z[c].got()
        lanes = slice(c * LANES, (c + 1) * LANES)
        proj_ref[:, lanes] = (fpart[c, x, 0].astype(F32) + fzgot[c].astype(F32)).astype(BF16)
        agrad_ref[:, lanes] = (bown[c] + bzgot[c].astype(F32)).astype(BF16)

    for w in zx + zc + xc0[0] + xc0[1] + xc1[0] + xc1[1] + w_c + w_d:
        w.sent()
    for w in f_x[0] + f_x[1] + f_z + b_z + g_d + g_c:
        w.sent()

    @pl.when(gives)
    def _():
        w_a.sent()
        g_b3.sent()

    @pl.when(keeps)
    def _():
        for w in [w_b1, w_b3, g_b1, g_a] + w_b2 + g_b2:
            w.sent()

    assert counter[0] <= N_WIRES


def on_device(attn_out, w_out, cotangent):
    tokens, block = attn_out.shape
    vmem = pl.BlockSpec(memory_space=pltpu.VMEM)
    rows = 2 * BLOCK

    def buf(*shape, dtype=BF16):
        return pltpu.VMEM(shape, dtype)

    proj, agrad, wgrad = pl.pallas_call(
        kernel,
        out_shape=(
            jax.ShapeDtypeStruct((block, tokens), BF16),
            jax.ShapeDtypeStruct((block, tokens), BF16),
            jax.ShapeDtypeStruct((SHARD, BLOCK), F32),
        ),
        in_specs=[vmem] * 3,
        out_specs=(vmem,) * 3,
        scratch_shapes=[
            buf(CHUNKS, 2, BLOCK, LANES),
            buf(CHUNKS, 4, 2, BLOCK, LANES),
            buf(4, 2, 2, 2, SHARD, rows),
            buf(SHARD, BLOCK),
            buf(SHARD, BLOCK),
            buf(rows, 4 * rows),
            buf(CHUNKS, 4, 2, BLOCK, LANES),
            buf(CHUNKS, 3, 2, BLOCK, LANES),
            buf(CHUNKS, BLOCK, LANES),
            buf(CHUNKS, BLOCK, LANES),
            buf(CHUNKS, BLOCK, LANES),
            buf(CHUNKS, BLOCK, LANES),
            buf(CHUNKS, BLOCK, LANES, dtype=F32),
            buf(4, 2, 2, 2, SHARD, rows),
            buf(4, 2, 2, SHARD, rows),
            buf(2, 2, 4, SHARD, rows),
            buf(3, 4, SHARD, rows),
            buf(4, SHARD, rows),
            buf(4, SHARD, rows),
            buf(2, SHARD, rows),
            buf(SHARD, rows),
            buf(SHARD, BLOCK),
            buf(SHARD, BLOCK),
            pltpu.SemaphoreType.DMA((N_WIRES,)),
            pltpu.SemaphoreType.DMA((N_WIRES,)),
        ],
        compiler_params=pltpu.CompilerParams(
            collective_id=0, has_side_effects=True, vmem_limit_bytes=48 * 2**20
        ),
    )(attn_out, w_out, cotangent)
    return proj.T, agrad.T, wgrad.T


def solution(mesh):
    return jax.shard_map(
        on_device,
        mesh=mesh,
        in_specs=(P("dp", "mp"), P("mp", "dp"), P("dp", "mp")),
        out_specs=(P("dp", "mp"), P("dp", "mp"), P("mp", "dp")),
        check_vma=False,
    )
```

```python
import jax
import jax.numpy as jnp
from jax import lax
from jax.experimental import pallas as pl
from jax.experimental.pallas import tpu as pltpu
from jax.sharding import PartitionSpec as P

BF16 = jnp.bfloat16
F32 = jnp.float32
CHUNKS = 2
LANES = 128
BLOCK = 192
SHARD = 48


def flip1(a):
    return a + 1 - 2 * (a % 2)


def flip4(a):
    return a + 4 - 8 * ((a // 4) % 2)


class Wire:
    def __init__(self, sems, index, arrives, src, dst, device):
        self.copy = pltpu.make_async_remote_copy(
            src_ref=src,
            dst_ref=dst,
            send_sem=sems[0].at[index],
            recv_sem=sems[1].at[arrives],
            device_id=device,
            device_id_type=pl.DeviceIdType.MESH,
        )
        self.leaves = False

    def start(self, only=None):
        self.leaves = True if only is None else only
        if only is None:
            self.copy.start()
        else:
            pl.when(only)(self.copy.start)
        return self

    def got(self, only=None):
        if only is None:
            self.copy.wait_recv()
        else:
            pl.when(only)(self.copy.wait_recv)

    def sent(self):
        if self.leaves is True:
            self.copy.wait_send()
        elif self.leaves is not False:
            pl.when(self.leaves)(self.copy.wait_send)


N_WIRES = 96
VMEM_LIMIT = 64 * 2**20 - 2**16


def kernel(
    x_ref, w_ref, g_ref,
    proj_ref, agrad_ref, wgrad_ref,
    xin, gin, xt, ct, wbuf, wown, wgot, wn,
    fpart, fgot, fsend, fzgot,
    bsend, bzgot, bown,
    gbuf, ggot, hbuf, hgot, ibuf, igot, tot, asend, agot,
    load_sem, send_sem, recv_sem,
):
    sems = (send_sem, recv_sem)
    counter, wires = [0], []
    dp = lax.axis_index("dp")
    mp = lax.axis_index("mp")
    x, zh = mp // 4, mp % 4
    zl, y, core = dp // 8, (dp // 2) % 4, dp % 2

    def device(x=x, zh=zh, zl=zl, y=y, core=core):
        return ((zl * 4 + y) * 2 + core, x * 4 + zh)

    def wire(src, dst, to, arrives=None):
        counter[0] += 1
        index = counter[0] - 1
        wires.append(Wire(sems, index, index if arrives is None else arrives, src, dst, to))
        return wires[-1]

    def reserve(n):
        counter[0] += n
        return counter[0] - n

    zn = flip1(zh)
    near, far, other = device(zh=zn), device(zh=3 - zh), device(core=1 - core)
    zl4 = flip4(zl)
    l4, near4 = device(zl=zl4), device(zh=zn, zl=zl4)
    x_to = [(x + d) % 4 for d in range(4)]
    y_to = [(y + d) % 4 for d in range(4)]
    pos, line = zl % 4, (zl // 4) * 4
    z_to = [device(zl=line + (pos + d) % 4) for d in range(4)]

    barrier = pltpu.get_barrier_semaphore()
    partners = [near, far, other, l4, near4] + z_to[1:]
    partners += [device(x=x_to[d]) for d in (1, 2, 3)]
    partners += [device(y=y_to[d]) for d in (1, 2, 3)]
    for partner in partners:
        pl.semaphore_signal(
            barrier, inc=1, device_id=partner, device_id_type=pl.DeviceIdType.MESH
        )

    loads = [
        pltpu.make_async_copy(src, dst, load_sem.at[i])
        for i, (src, dst) in enumerate(((x_ref, xin), (g_ref, gin), (w_ref, wown)))
    ]
    for load in loads:
        load.start()

    za, zb = zh // 2, zh % 2

    def place(yy):
        return (yy // 2 + zb) % 2, yy % 2

    def parity(yy):
        return (za + place(yy)[0]) % 2

    def first(yy):
        away = (zl + parity(yy)) % 2
        return ((pos + 3 * away) % 4) // 2

    sel, half = place(y)
    par = parity(y)
    keeps = (zl % 2) == par
    gives = (zl % 2) != par
    khi, klo = zl // 4, (zl // 2) % 2

    for load in loads:
        load.wait()
    for c in range(CHUNKS):
        xt[c, 0] = xin[:, c * LANES:(c + 1) * LANES]
        ct[c, x, 0] = gin[:, c * LANES:(c + 1) * LANES]

    pl.semaphore_wait(barrier, len(partners))

    w_a = [wire(wown, wgot.at[i], to) for i, to in enumerate((near, near4, l4))]

    zx = [wire(xt.at[c, 0], xt.at[c, 1], near) for c in range(CHUNKS)]
    zc = [wire(ct.at[c, x, 0], ct.at[c, x, 1], far) for c in range(CHUNKS)]
    xc0 = [
        [wire(ct.at[c, x, 0], ct.at[c, x, 0], device(x=x_to[d])) for d in (1, 2, 3)]
        for c in range(CHUNKS)
    ]
    xc1 = [
        [wire(ct.at[c, x, 1], ct.at[c, x, 1], device(x=x_to[d])) for d in (1, 2, 3)]
        for c in range(CHUNKS)
    ]

    def pair(low, yy):
        s, h = place(yy)
        return wbuf.at[:, low, s, h, core]

    one = first(y)
    lows = (one, 1 - one)
    w_b = [None] + [wire(pair(klo, y), pair(klo, y), z_to[d]) for d in (1, 2, 3)]
    w_c = [
        [wire(pair(low, y), pair(low, y), device(y=y_to[d])) for d in (1, 2, 3)]
        for low in lows
    ]
    w_d = [[], []]
    for d in range(4):
        yy = (y + 4 - d) % 4
        for i in range(2):
            low = first(yy) if i == 0 else 1 - first(yy)
            w_d[i].append(wire(pair(low, yy), pair(low, yy), other))

    def weights_a():
        w_a[0].start(gives)
        w_a[1].start(gives)
        w_a[2].start(keeps)

    def weights_line():
        @pl.when(keeps)
        def _():
            for w in w_a:
                w.got()
            wbuf[khi, klo, sel, half, core] = jnp.concatenate([wown[...], wgot[0]], axis=1)
            wbuf[1 - khi, klo, sel, half, core] = jnp.concatenate([wgot[2], wgot[1]], axis=1)

        for d in (1, 3, 2):
            w_b[d].start(keeps)

    def weights_y(i):
        if i == 0:
            w_b[1].got(gives)
        else:
            w_b[2].got(keeps)
            w_b[3].got(gives)
        for w in w_c[i] + [w_d[i][0]]:
            w.start()

    def weights_core(i):
        for d in (1, 2, 3):
            w_c[i][d - 1].got()
            w_d[i][d].start()

    def weights_end():
        for i in range(2):
            for d in range(4):
                w_d[i][d].got()
        for kk in range(4):
            wn[:, kk * rows:(kk + 1) * rows] = weights(kk).T

    def gather_z(c, only=None):
        zx[c].start(only)
        zc[c].start(only)

    def gather_x0():
        for c in range(CHUNKS):
            for w in xc0[c]:
                w.start()

    def gather_x1(c):
        zc[c].got()
        for w in xc1[c]:
            w.start()

    rows = 2 * BLOCK

    def weights(kk):
        return wbuf[kk // 2, kk % 2].reshape(rows, rows)

    f_x, f_z, b_z = [], [], []

    def gathered(c):
        zx[c].got()
        for w in xc0[c] + xc1[c]:
            w.got()

    def forward(c):
        xval = xt[c].reshape(rows, LANES)
        for kk in range(4):
            part = jnp.dot(weights(kk), xval, preferred_element_type=F32)
            fpart[c, kk] = part.astype(BF16).reshape(2, BLOCK, LANES)
        f_x.append([
            wire(fpart.at[c, x_to[d]], fgot.at[c, d - 1], device(x=x_to[d])).start()
            for d in (1, 2, 3)
        ])

    def backward(c):
        part = jnp.dot(wn[...], ct[c].reshape(4 * rows, LANES), preferred_element_type=F32)
        bown[c] = part[:BLOCK]
        bsend[c] = part[BLOCK:].astype(BF16)
        b_z.append(wire(bsend.at[c], bzgot.at[c], near))

    def forward_sum(c):
        for w in f_x[c]:
            w.got()
        total = fpart[c, x].astype(F32)
        for d in range(3):
            total += fgot[c, d].astype(F32)
        fsend[c] = total[1].astype(BF16)
        f_z.append(wire(fsend.at[c], fzgot.at[c], far))
        fpart[c, x, 0] = total[0].astype(BF16)

    g_d = [None] * 4

    def gradient(low):
        for kk in (low, low + 2):
            part = jnp.zeros((rows, rows), F32)
            for c in range(CHUNKS):
                part += lax.dot_general(
                    ct[c, kk].reshape(rows, LANES), xt[c].reshape(rows, LANES),
                    (((1,), (1,)), ((), ())), preferred_element_type=F32,
                )
            gbuf[kk] = part.astype(BF16).reshape(2, 2, 2, SHARD, rows)
            g_d[kk] = wire(gbuf.at[kk, :, :, 1 - core], ggot.at[kk], other).start()

    g_c = [[], []]

    def gradient_y(low):
        for i in range(2):
            kk = low + 2 * i
            g_d[kk].got()
            hbuf[low, :, :, i] = (
                gbuf[kk, :, :, core].astype(F32) + ggot[kk].astype(F32)
            ).astype(BF16)
        for d in (1, 2, 3):
            s, h = place(y_to[d])
            g_c[low].append(
                wire(hbuf.at[low, s, h], hgot.at[low, d - 1], device(y=y_to[d])).start()
            )

    g_b_base = reserve(3)
    g_b = [None, None]

    def gradient_z(low):
        for w in g_c[low]:
            w.got()
        total = hbuf[low, sel, half].astype(F32)
        for d in range(3):
            total += hgot[low, d].astype(F32)
        ibuf[low] = total.astype(BF16)
        goal = 2 * low + par
        step = (goal + 4 - pos) % 4
        slot = (step + 3) % 4
        slot = slot - slot // 3
        g_b[low] = wire(ibuf.at[low], igot.at[slot], device(zl=line + goal), g_b_base + slot)
        g_b[low].start(step != 0)

    g_b_in = [wire(ibuf.at[0], igot.at[d], other, g_b_base + d) for d in range(3)]
    g_a = [wire(asend.at[i], agot.at[i], to) for i, to in enumerate((near, near4, l4))]

    def gradient_sum():
        @pl.when(keeps)
        def _():
            for w in g_b_in:
                w.got()
            total = ibuf[klo].astype(F32)
            for d in range(3):
                total += igot[d].astype(F32)
            tot[...] = total
            asend[0] = tot[khi][:, BLOCK:].astype(BF16)
            asend[1] = tot[1 - khi][:, BLOCK:].astype(BF16)
            asend[2] = tot[1 - khi][:, :BLOCK].astype(BF16)

        for w in (g_a[1], g_a[0], g_a[2]):
            w.start(keeps)

    def gradient_end():
        @pl.when(keeps)
        def _():
            g_a[2].got()
            wgrad_ref[...] = tot[khi][:, :BLOCK] + agot[2].astype(F32)

        @pl.when(gives)
        def _():
            g_a[0].got()
            g_a[1].got()
            wgrad_ref[...] = agot[0].astype(F32) + agot[1].astype(F32)

    def finish(c):
        f_z[c].got()
        b_z[c].got()
        lanes = slice(c * LANES, (c + 1) * LANES)
        proj_ref[:, lanes] = (fpart[c, x, 0].astype(F32) + fzgot[c].astype(F32)).astype(BF16)
        agrad_ref[:, lanes] = (bown[c] + bzgot[c].astype(F32)).astype(BF16)

    weights_a()
    gather_z(0)
    gather_z(1)
    gather_x0()
    weights_line()
    weights_y(0)
    gather_x1(0)
    weights_y(1)
    gather_x1(1)
    weights_core(0)
    weights_core(1)
    gathered(0)
    gathered(1)
    gradient(0)
    gradient(1)
    weights_end()
    backward(0)
    b_z[0].start()
    forward(0)
    gradient_y(0)
    gradient_y(1)
    forward_sum(0)
    f_z[0].start()
    backward(1)
    forward(1)
    gradient_z(0)
    gradient_z(1)
    b_z[1].start()
    forward_sum(1)
    f_z[1].start()
    gradient_sum()
    finish(0)
    finish(1)
    gradient_end()

    for w in wires:
        w.sent()

    assert counter[0] <= N_WIRES


def on_device(attn_out, w_out, cotangent):
    tokens, block = attn_out.shape
    vmem = pl.BlockSpec(memory_space=pltpu.VMEM)
    rows = 2 * BLOCK

    def buf(*shape, dtype=BF16):
        return pltpu.VMEM(shape, dtype)

    proj, agrad, wgrad = pl.pallas_call(
        kernel,
        out_shape=(
            jax.ShapeDtypeStruct((block, tokens), BF16),
            jax.ShapeDtypeStruct((block, tokens), BF16),
            jax.ShapeDtypeStruct((SHARD, BLOCK), F32),
        ),
        in_specs=[pl.BlockSpec(memory_space=pltpu.HBM)] * 3,
        out_specs=(vmem,) * 3,
        scratch_shapes=[
            buf(BLOCK, tokens),
            buf(BLOCK, tokens),
            buf(CHUNKS, 2, BLOCK, LANES),
            buf(CHUNKS, 4, 2, BLOCK, LANES),
            buf(2, 2, 2, 2, 2, SHARD, rows),
            buf(SHARD, BLOCK),
            buf(3, SHARD, BLOCK),
            buf(rows, 4 * rows),
            buf(CHUNKS, 4, 2, BLOCK, LANES),
            buf(CHUNKS, 3, 2, BLOCK, LANES),
            buf(CHUNKS, BLOCK, LANES),
            buf(CHUNKS, BLOCK, LANES),
            buf(CHUNKS, BLOCK, LANES),
            buf(CHUNKS, BLOCK, LANES),
            buf(CHUNKS, BLOCK, LANES, dtype=F32),
            buf(4, 2, 2, 2, SHARD, rows),
            buf(4, 2, 2, SHARD, rows),
            buf(2, 2, 2, 2, SHARD, rows),
            buf(2, 3, 2, SHARD, rows),
            buf(2, 2, SHARD, rows),
            buf(3, 2, SHARD, rows),
            buf(2, SHARD, rows, dtype=F32),
            buf(3, SHARD, BLOCK),
            buf(3, SHARD, BLOCK),
            pltpu.SemaphoreType.DMA((3,)),
            pltpu.SemaphoreType.DMA((N_WIRES,)),
            pltpu.SemaphoreType.DMA((N_WIRES,)),
        ],
        compiler_params=pltpu.CompilerParams(
            collective_id=0, has_side_effects=True, vmem_limit_bytes=VMEM_LIMIT
        ),
    )(attn_out.T, w_out.T, cotangent.T)
    return proj.T, agrad.T, wgrad.T


def solution(mesh):
    return jax.shard_map(
        on_device,
        mesh=mesh,
        in_specs=(P("dp", "mp"), P("mp", "dp"), P("dp", "mp")),
        out_specs=(P("dp", "mp"), P("dp", "mp"), P("mp", "dp")),
        check_vma=False,
    )
```

```python
import jax
import jax.numpy as jnp
from jax import lax
from jax.experimental import pallas as pl
from jax.experimental.pallas import tpu as pltpu
from jax.sharding import PartitionSpec as P

BF16 = jnp.bfloat16
F32 = jnp.float32
CHUNKS = 2
LANES = 128
BLOCK = 192
SHARD = 48


def flip1(a):
    return a + 1 - 2 * (a % 2)


def flip4(a):
    return a + 4 - 8 * ((a // 4) % 2)


class Wire:
    def __init__(self, sems, index, arrives, src, dst, device):
        self.copy = pltpu.make_async_remote_copy(
            src_ref=src,
            dst_ref=dst,
            send_sem=sems[0].at[index],
            recv_sem=sems[1].at[arrives],
            device_id=device,
            device_id_type=pl.DeviceIdType.MESH,
        )
        self.leaves = False

    def start(self, only=None):
        self.leaves = True if only is None else only
        if only is None:
            self.copy.start()
        else:
            pl.when(only)(self.copy.start)
        return self

    def got(self, only=None):
        if only is None:
            self.copy.wait_recv()
        else:
            pl.when(only)(self.copy.wait_recv)

    def sent(self):
        if self.leaves is True:
            self.copy.wait_send()
        elif self.leaves is not False:
            pl.when(self.leaves)(self.copy.wait_send)


N_WIRES = 96
VMEM_LIMIT = 64 * 2**20 - 2**16


def kernel(
    x_ref, w_ref, g_ref,
    proj_ref, agrad_ref, wgrad_ref,
    xin, gin, xt, ct, wbuf, wown, wgot, wn,
    fpart, fgot, fsend, fzgot,
    bsend, bzgot, bown,
    gbuf, ggot, hbuf, hgot, ibuf, igot, tot, asend, agot,
    load_sem, send_sem, recv_sem,
):
    sems = (send_sem, recv_sem)
    counter, wires = [0], []
    dp = lax.axis_index("dp")
    mp = lax.axis_index("mp")
    x, zh = mp // 4, mp % 4
    zl, y, core = dp // 8, (dp // 2) % 4, dp % 2

    def device(x=x, zh=zh, zl=zl, y=y, core=core):
        return ((zl * 4 + y) * 2 + core, x * 4 + zh)

    def wire(src, dst, to, arrives=None):
        counter[0] += 1
        index = counter[0] - 1
        wires.append(Wire(sems, index, index if arrives is None else arrives, src, dst, to))
        return wires[-1]

    def reserve(n):
        counter[0] += n
        return counter[0] - n

    zn = flip1(zh)
    near, far, other = device(zh=zn), device(zh=3 - zh), device(core=1 - core)
    zl4 = flip4(zl)
    l4, near4 = device(zl=zl4), device(zh=zn, zl=zl4)
    x_to = [(x + d) % 4 for d in range(4)]
    y_to = [(y + d) % 4 for d in range(4)]
    pos, line = zl % 4, (zl // 4) * 4
    z_to = [device(zl=line + (pos + d) % 4) for d in range(4)]

    barrier = pltpu.get_barrier_semaphore()
    partners = [near, far, other, l4, near4] + z_to[1:]
    partners += [device(x=x_to[d]) for d in (1, 2, 3)]
    partners += [device(y=y_to[d]) for d in (1, 2, 3)]
    for partner in partners:
        pl.semaphore_signal(
            barrier, inc=1, device_id=partner, device_id_type=pl.DeviceIdType.MESH
        )

    loads = [
        pltpu.make_async_copy(src, dst, load_sem.at[i])
        for i, (src, dst) in enumerate(((x_ref, xin), (g_ref, gin), (w_ref, wown)))
    ]
    for load in loads:
        load.start()

    za, zb = zh // 2, zh % 2

    def place(yy):
        return (yy // 2 + zb) % 2, yy % 2

    def parity(yy):
        return (za + place(yy)[0]) % 2

    def first(yy):
        away = (zl + parity(yy)) % 2
        return ((pos + 3 * away) % 4) // 2

    sel, half = place(y)
    par = parity(y)
    keeps = (zl % 2) == par
    gives = (zl % 2) != par
    khi, klo = zl // 4, (zl // 2) % 2

    for load in loads:
        load.wait()
    for c in range(CHUNKS):
        xt[c, 0] = xin[:, c * LANES:(c + 1) * LANES]
        ct[c, x, 0] = gin[:, c * LANES:(c + 1) * LANES]

    pl.semaphore_wait(barrier, len(partners))

    w_a = [wire(wown, wgot.at[i], to) for i, to in enumerate((near, near4, l4))]

    zx = [wire(xt.at[c, 0], xt.at[c, 1], near) for c in range(CHUNKS)]
    zc = [wire(ct.at[c, x, 0], ct.at[c, x, 1], far) for c in range(CHUNKS)]
    xc0 = [
        [wire(ct.at[c, x, 0], ct.at[c, x, 0], device(x=x_to[d])) for d in (1, 2, 3)]
        for c in range(CHUNKS)
    ]
    xc1 = [
        [wire(ct.at[c, x, 1], ct.at[c, x, 1], device(x=x_to[d])) for d in (1, 2, 3)]
        for c in range(CHUNKS)
    ]

    def pair(low, yy):
        s, h = place(yy)
        return wbuf.at[:, low, s, h, core]

    one = first(y)
    lows = (one, 1 - one)
    w_b = [None] + [wire(pair(klo, y), pair(klo, y), z_to[d]) for d in (1, 2, 3)]
    w_c = [
        [wire(pair(low, y), pair(low, y), device(y=y_to[d])) for d in (1, 2, 3)]
        for low in lows
    ]
    w_d = [[], []]
    for d in range(4):
        yy = (y + 4 - d) % 4
        for i in range(2):
            low = first(yy) if i == 0 else 1 - first(yy)
            w_d[i].append(wire(pair(low, yy), pair(low, yy), other))

    def weights_a():
        w_a[0].start(gives)
        w_a[1].start(gives)
        w_a[2].start(keeps)

    def weights_line():
        @pl.when(keeps)
        def _():
            for w in w_a:
                w.got()
            wbuf[khi, klo, sel, half, core] = jnp.concatenate([wown[...], wgot[0]], axis=1)
            wbuf[1 - khi, klo, sel, half, core] = jnp.concatenate([wgot[2], wgot[1]], axis=1)

        for d in (1, 3, 2):
            w_b[d].start(keeps)

    def weights_y(i):
        if i == 0:
            w_b[1].got(gives)
        else:
            w_b[2].got(keeps)
            w_b[3].got(gives)
        for w in w_c[i] + [w_d[i][0]]:
            w.start()

    def weights_core(i):
        for d in (1, 2, 3):
            w_c[i][d - 1].got()
            w_d[i][d].start()

    def weights_end():
        for i in range(2):
            for d in range(4):
                w_d[i][d].got()
        for kk in range(4):
            wn[:, kk * rows:(kk + 1) * rows] = weights(kk).T

    def gather_z(c, only=None):
        zx[c].start(only)
        zc[c].start(only)

    def gather_x0():
        for c in range(CHUNKS):
            for w in xc0[c]:
                w.start()

    def gather_x1(c):
        zc[c].got()
        for w in xc1[c]:
            w.start()

    rows = 2 * BLOCK

    def weights(kk):
        return wbuf[kk // 2, kk % 2].reshape(rows, rows)

    f_x, f_z, b_z = [], [], []

    def gathered(c):
        zx[c].got()
        for w in xc0[c] + xc1[c]:
            w.got()

    def forward(c):
        xval = xt[c].reshape(rows, LANES)
        for kk in range(4):
            part = jnp.dot(weights(kk), xval, preferred_element_type=F32)
            fpart[c, kk] = part.astype(BF16).reshape(2, BLOCK, LANES)
        f_x.append([
            wire(fpart.at[c, x_to[d]], fgot.at[c, d - 1], device(x=x_to[d])).start()
            for d in (1, 2, 3)
        ])

    def backward(c):
        part = jnp.dot(wn[...], ct[c].reshape(4 * rows, LANES), preferred_element_type=F32)
        bown[c] = part[:BLOCK]
        bsend[c] = part[BLOCK:].astype(BF16)
        b_z.append(wire(bsend.at[c], bzgot.at[c], near))

    def forward_sum(c):
        for w in f_x[c]:
            w.got()
        total = fpart[c, x].astype(F32)
        for d in range(3):
            total += fgot[c, d].astype(F32)
        fsend[c] = total[1].astype(BF16)
        f_z.append(wire(fsend.at[c], fzgot.at[c], far))
        fpart[c, x, 0] = total[0].astype(BF16)

    g_d = [None] * 4

    def gradient(low):
        for kk in (low, low + 2):
            part = jnp.zeros((rows, rows), F32)
            for c in range(CHUNKS):
                part += lax.dot_general(
                    ct[c, kk].reshape(rows, LANES), xt[c].reshape(rows, LANES),
                    (((1,), (1,)), ((), ())), preferred_element_type=F32,
                )
            gbuf[kk] = part.astype(BF16).reshape(2, 2, 2, SHARD, rows)
            g_d[kk] = wire(gbuf.at[kk, :, :, 1 - core], ggot.at[kk], other).start()

    g_c = [[], []]

    def gradient_y(low):
        for i in range(2):
            kk = low + 2 * i
            g_d[kk].got()
            hbuf[low, :, :, i] = (
                gbuf[kk, :, :, core].astype(F32) + ggot[kk].astype(F32)
            ).astype(BF16)
        for d in (1, 2, 3):
            s, h = place(y_to[d])
            g_c[low].append(
                wire(hbuf.at[low, s, h], hgot.at[low, d - 1], device(y=y_to[d])).start()
            )

    g_b_base = reserve(3)
    g_b = [None, None]

    def gradient_z(low):
        for w in g_c[low]:
            w.got()
        total = hbuf[low, sel, half].astype(F32)
        for d in range(3):
            total += hgot[low, d].astype(F32)
        ibuf[low] = total.astype(BF16)
        goal = 2 * low + par
        step = (goal + 4 - pos) % 4
        slot = (step + 3) % 4
        slot = slot - slot // 3
        g_b[low] = wire(ibuf.at[low], igot.at[slot], device(zl=line + goal), g_b_base + slot)
        g_b[low].start(step != 0)

    g_b_in = [wire(ibuf.at[0], igot.at[d], other, g_b_base + d) for d in range(3)]
    g_a = [wire(asend.at[i], agot.at[i], to) for i, to in enumerate((near, near4, l4))]

    def gradient_sum():
        @pl.when(keeps)
        def _():
            for w in g_b_in:
                w.got()
            total = ibuf[klo].astype(F32)
            for d in range(3):
                total += igot[d].astype(F32)
            tot[...] = total
            asend[0] = tot[khi][:, BLOCK:].astype(BF16)
            asend[1] = tot[1 - khi][:, BLOCK:].astype(BF16)
            asend[2] = tot[1 - khi][:, :BLOCK].astype(BF16)

        for w in (g_a[1], g_a[0], g_a[2]):
            w.start(keeps)

    def gradient_end():
        @pl.when(keeps)
        def _():
            g_a[2].got()
            wgrad_ref[...] = tot[khi][:, :BLOCK] + agot[2].astype(F32)

        @pl.when(gives)
        def _():
            g_a[0].got()
            g_a[1].got()
            wgrad_ref[...] = agot[0].astype(F32) + agot[1].astype(F32)

    def finish(c):
        f_z[c].got()
        b_z[c].got()
        lanes = slice(c * LANES, (c + 1) * LANES)
        proj_ref[:, lanes] = (fpart[c, x, 0].astype(F32) + fzgot[c].astype(F32)).astype(BF16)
        agrad_ref[:, lanes] = (bown[c] + bzgot[c].astype(F32)).astype(BF16)

    weights_a()
    gather_z(0)
    gather_z(1)
    gather_x0()
    weights_line()
    weights_y(0)
    gather_x1(0)
    weights_y(1)
    gather_x1(1)
    weights_core(0)
    weights_core(1)
    gathered(0)
    gathered(1)
    gradient(0)
    gradient(1)
    weights_end()
    forward(0)
    forward(1)
    backward(0)
    b_z[0].start()
    gradient_y(0)
    gradient_y(1)
    forward_sum(0)
    f_z[0].start()
    backward(1)
    gradient_z(0)
    gradient_z(1)
    b_z[1].start()
    forward_sum(1)
    f_z[1].start()
    gradient_sum()
    finish(0)
    finish(1)
    gradient_end()

    for w in wires:
        w.sent()

    assert counter[0] <= N_WIRES


def on_device(attn_out, w_out, cotangent):
    tokens, block = attn_out.shape
    vmem = pl.BlockSpec(memory_space=pltpu.VMEM)
    rows = 2 * BLOCK

    def buf(*shape, dtype=BF16):
        return pltpu.VMEM(shape, dtype)

    proj, agrad, wgrad = pl.pallas_call(
        kernel,
        out_shape=(
            jax.ShapeDtypeStruct((block, tokens), BF16),
            jax.ShapeDtypeStruct((block, tokens), BF16),
            jax.ShapeDtypeStruct((SHARD, BLOCK), F32),
        ),
        in_specs=[pl.BlockSpec(memory_space=pltpu.HBM)] * 3,
        out_specs=(vmem,) * 3,
        scratch_shapes=[
            buf(BLOCK, tokens),
            buf(BLOCK, tokens),
            buf(CHUNKS, 2, BLOCK, LANES),
            buf(CHUNKS, 4, 2, BLOCK, LANES),
            buf(2, 2, 2, 2, 2, SHARD, rows),
            buf(SHARD, BLOCK),
            buf(3, SHARD, BLOCK),
            buf(rows, 4 * rows),
            buf(CHUNKS, 4, 2, BLOCK, LANES),
            buf(CHUNKS, 3, 2, BLOCK, LANES),
            buf(CHUNKS, BLOCK, LANES),
            buf(CHUNKS, BLOCK, LANES),
            buf(CHUNKS, BLOCK, LANES),
            buf(CHUNKS, BLOCK, LANES),
            buf(CHUNKS, BLOCK, LANES, dtype=F32),
            buf(4, 2, 2, 2, SHARD, rows),
            buf(4, 2, 2, SHARD, rows),
            buf(2, 2, 2, 2, SHARD, rows),
            buf(2, 3, 2, SHARD, rows),
            buf(2, 2, SHARD, rows),
            buf(3, 2, SHARD, rows),
            buf(2, SHARD, rows, dtype=F32),
            buf(3, SHARD, BLOCK),
            buf(3, SHARD, BLOCK),
            pltpu.SemaphoreType.DMA((3,)),
            pltpu.SemaphoreType.DMA((N_WIRES,)),
            pltpu.SemaphoreType.DMA((N_WIRES,)),
        ],
        compiler_params=pltpu.CompilerParams(
            collective_id=0, has_side_effects=True, vmem_limit_bytes=VMEM_LIMIT
        ),
    )(attn_out.T, w_out.T, cotangent.T)
    return proj.T, agrad.T, wgrad.T


def solution(mesh):
    return jax.shard_map(
        on_device,
        mesh=mesh,
        in_specs=(P("dp", "mp"), P("mp", "dp"), P("dp", "mp")),
        out_specs=(P("dp", "mp"), P("dp", "mp"), P("mp", "dp")),
        check_vma=False,
    )
```

```python
import jax
import jax.numpy as jnp
from jax import lax
from jax.experimental import pallas as pl
from jax.experimental.pallas import tpu as pltpu
from jax.sharding import PartitionSpec as P

BF16 = jnp.bfloat16
F32 = jnp.float32
CHUNKS = 2
LANES = 128
BLOCK = 192
SHARD = 48


def flip1(a):
    return a + 1 - 2 * (a % 2)


def flip4(a):
    return a + 4 - 8 * ((a // 4) % 2)


class Wire:
    def __init__(self, sems, index, arrives, src, dst, device):
        self.copy = pltpu.make_async_remote_copy(
            src_ref=src,
            dst_ref=dst,
            send_sem=sems[0].at[index],
            recv_sem=sems[1].at[arrives],
            device_id=device,
            device_id_type=pl.DeviceIdType.MESH,
        )
        self.leaves = False

    def start(self, only=None):
        self.leaves = True if only is None else only
        if only is None:
            self.copy.start()
        else:
            pl.when(only)(self.copy.start)
        return self

    def got(self, only=None):
        if only is None:
            self.copy.wait_recv()
        else:
            pl.when(only)(self.copy.wait_recv)

    def sent(self):
        if self.leaves is True:
            self.copy.wait_send()
        elif self.leaves is not False:
            pl.when(self.leaves)(self.copy.wait_send)


N_WIRES = 96
VMEM_LIMIT = 64 * 2**20 - 2**16


def kernel(
    x_ref, w_ref, g_ref,
    proj_ref, agrad_ref, wgrad_ref,
    xin, gin, xt, ct, wbuf, wown, wgot, wn,
    fpart, fgot, fsend, fzgot,
    bsend, bzgot, bown,
    gbuf, ggot, hbuf, hgot, ibuf, igot, tot, asend, agot,
    load_sem, send_sem, recv_sem,
):
    sems = (send_sem, recv_sem)
    counter, wires = [0], []
    dp = lax.axis_index("dp")
    mp = lax.axis_index("mp")
    x, zh = mp // 4, mp % 4
    zl, y, core = dp // 8, (dp // 2) % 4, dp % 2

    def device(x=x, zh=zh, zl=zl, y=y, core=core):
        return ((zl * 4 + y) * 2 + core, x * 4 + zh)

    def wire(src, dst, to, arrives=None):
        counter[0] += 1
        index = counter[0] - 1
        wires.append(Wire(sems, index, index if arrives is None else arrives, src, dst, to))
        return wires[-1]

    def reserve(n):
        counter[0] += n
        return counter[0] - n

    zn = flip1(zh)
    near, far, other = device(zh=zn), device(zh=3 - zh), device(core=1 - core)
    zl4 = flip4(zl)
    l4, near4 = device(zl=zl4), device(zh=zn, zl=zl4)
    x_to = [(x + d) % 4 for d in range(4)]
    y_to = [(y + d) % 4 for d in range(4)]
    pos, line = zl % 4, (zl // 4) * 4
    z_to = [device(zl=line + (pos + d) % 4) for d in range(4)]

    barrier = pltpu.get_barrier_semaphore()
    partners = [near, far, other, l4, near4] + z_to[1:]
    partners += [device(x=x_to[d]) for d in (1, 2, 3)]
    partners += [device(y=y_to[d]) for d in (1, 2, 3)]
    for partner in partners:
        pl.semaphore_signal(
            barrier, inc=1, device_id=partner, device_id_type=pl.DeviceIdType.MESH
        )

    loads = [
        pltpu.make_async_copy(src, dst, load_sem.at[i])
        for i, (src, dst) in enumerate(((x_ref, xin), (g_ref, gin), (w_ref, wown)))
    ]
    for load in loads:
        load.start()

    za, zb = zh // 2, zh % 2

    def place(yy):
        return (yy // 2 + zb) % 2, yy % 2

    def parity(yy):
        return (za + place(yy)[0]) % 2

    def first(yy):
        away = (zl + parity(yy)) % 2
        return ((pos + 3 * away) % 4) // 2

    sel, half = place(y)
    par = parity(y)
    keeps = (zl % 2) == par
    gives = (zl % 2) != par
    khi, klo = zl // 4, (zl // 2) % 2

    for load in loads:
        load.wait()
    for c in range(CHUNKS):
        xt[c, 0] = xin[:, c * LANES:(c + 1) * LANES]
        ct[c, x, 0] = gin[:, c * LANES:(c + 1) * LANES]

    pl.semaphore_wait(barrier, len(partners))

    w_a = [wire(wown, wgot.at[i], to) for i, to in enumerate((near, near4, l4))]

    zx = [wire(xt.at[c, 0], xt.at[c, 1], near) for c in range(CHUNKS)]
    zc = [wire(ct.at[c, x, 0], ct.at[c, x, 1], far) for c in range(CHUNKS)]
    xc0 = [
        [wire(ct.at[c, x, 0], ct.at[c, x, 0], device(x=x_to[d])) for d in (1, 2, 3)]
        for c in range(CHUNKS)
    ]
    xc1 = [
        [wire(ct.at[c, x, 1], ct.at[c, x, 1], device(x=x_to[d])) for d in (1, 2, 3)]
        for c in range(CHUNKS)
    ]

    def pair(low, yy):
        s, h = place(yy)
        return wbuf.at[:, low, s, h, core]

    one = first(y)
    lows = (one, 1 - one)
    w_b = [None] + [wire(pair(klo, y), pair(klo, y), z_to[d]) for d in (1, 2, 3)]
    w_c = [
        [wire(pair(low, y), pair(low, y), device(y=y_to[d])) for d in (1, 2, 3)]
        for low in lows
    ]
    w_d = [[], []]
    for d in range(4):
        yy = (y + 4 - d) % 4
        for i in range(2):
            low = first(yy) if i == 0 else 1 - first(yy)
            w_d[i].append(wire(pair(low, yy), pair(low, yy), other))

    def weights_a():
        w_a[0].start(gives)
        w_a[1].start(gives)
        w_a[2].start(keeps)

    def weights_line():
        @pl.when(keeps)
        def _():
            for w in w_a:
                w.got()
            wbuf[khi, klo, sel, half, core] = jnp.concatenate([wown[...], wgot[0]], axis=1)
            wbuf[1 - khi, klo, sel, half, core] = jnp.concatenate([wgot[2], wgot[1]], axis=1)

        for d in (1, 3, 2):
            w_b[d].start(keeps)

    def weights_y(i):
        if i == 0:
            w_b[1].got(gives)
        else:
            w_b[2].got(keeps)
            w_b[3].got(gives)
        for w in w_c[i] + [w_d[i][0]]:
            w.start()

    def weights_core(i):
        for d in (1, 2, 3):
            w_c[i][d - 1].got()
            w_d[i][d].start()

    def weights_end():
        for i in range(2):
            for d in range(4):
                w_d[i][d].got()
        for kk in range(4):
            wn[:, kk * rows:(kk + 1) * rows] = weights(kk).T

    def gather_z(c, only=None):
        zx[c].start(only)
        zc[c].start(only)

    def gather_x0():
        for c in range(CHUNKS):
            for w in xc0[c]:
                w.start()

    def gather_x1(c):
        zc[c].got()
        for w in xc1[c]:
            w.start()

    rows = 2 * BLOCK

    def weights(kk):
        return wbuf[kk // 2, kk % 2].reshape(rows, rows)

    f_x, f_z, b_z = [], [], []

    def gathered(c):
        zx[c].got()
        for w in xc0[c] + xc1[c]:
            w.got()

    def forward(c):
        xval = xt[c].reshape(rows, LANES)
        for kk in range(4):
            part = jnp.dot(weights(kk), xval, preferred_element_type=F32)
            fpart[c, kk] = part.astype(BF16).reshape(2, BLOCK, LANES)
        f_x.append([
            wire(fpart.at[c, x_to[d]], fgot.at[c, d - 1], device(x=x_to[d])).start()
            for d in (1, 2, 3)
        ])

    def backward(c):
        part = jnp.dot(wn[...], ct[c].reshape(4 * rows, LANES), preferred_element_type=F32)
        bown[c] = part[:BLOCK]
        bsend[c] = part[BLOCK:].astype(BF16)
        b_z.append(wire(bsend.at[c], bzgot.at[c], near))

    def forward_sum(c):
        for w in f_x[c]:
            w.got()
        total = fpart[c, x].astype(F32)
        for d in range(3):
            total += fgot[c, d].astype(F32)
        fsend[c] = total[1].astype(BF16)
        f_z.append(wire(fsend.at[c], fzgot.at[c], far))
        fpart[c, x, 0] = total[0].astype(BF16)

    g_d = [None] * 4

    def gradient(low):
        for kk in (low, low + 2):
            part = jnp.zeros((rows, rows), F32)
            for c in range(CHUNKS):
                part += lax.dot_general(
                    ct[c, kk].reshape(rows, LANES), xt[c].reshape(rows, LANES),
                    (((1,), (1,)), ((), ())), preferred_element_type=F32,
                )
            gbuf[kk] = part.astype(BF16).reshape(2, 2, 2, SHARD, rows)
            g_d[kk] = wire(gbuf.at[kk, :, :, 1 - core], ggot.at[kk], other).start()

    g_c = [[], []]

    def gradient_y(low):
        for i in range(2):
            kk = low + 2 * i
            g_d[kk].got()
            hbuf[low, :, :, i] = (
                gbuf[kk, :, :, core].astype(F32) + ggot[kk].astype(F32)
            ).astype(BF16)
        for d in (1, 2, 3):
            s, h = place(y_to[d])
            g_c[low].append(
                wire(hbuf.at[low, s, h], hgot.at[low, d - 1], device(y=y_to[d])).start()
            )

    g_b_base = reserve(3)
    g_b = [None, None]

    def gradient_z(low):
        for w in g_c[low]:
            w.got()
        total = hbuf[low, sel, half].astype(F32)
        for d in range(3):
            total += hgot[low, d].astype(F32)
        ibuf[low] = total.astype(BF16)
        goal = 2 * low + par
        step = (goal + 4 - pos) % 4
        slot = (step + 3) % 4
        slot = slot - slot // 3
        g_b[low] = wire(ibuf.at[low], igot.at[slot], device(zl=line + goal), g_b_base + slot)
        g_b[low].start(step != 0)

    g_b_in = [wire(ibuf.at[0], igot.at[d], other, g_b_base + d) for d in range(3)]
    g_a = [wire(asend.at[i], agot.at[i], to) for i, to in enumerate((near, near4, l4))]

    def gradient_sum():
        @pl.when(keeps)
        def _():
            for w in g_b_in:
                w.got()
            total = ibuf[klo].astype(F32)
            for d in range(3):
                total += igot[d].astype(F32)
            tot[...] = total
            asend[0] = tot[khi][:, BLOCK:].astype(BF16)
            asend[1] = tot[1 - khi][:, BLOCK:].astype(BF16)
            asend[2] = tot[1 - khi][:, :BLOCK].astype(BF16)

        for w in (g_a[1], g_a[0], g_a[2]):
            w.start(keeps)

    def gradient_end():
        @pl.when(keeps)
        def _():
            g_a[2].got()
            wgrad_ref[...] = tot[khi][:, :BLOCK] + agot[2].astype(F32)

        @pl.when(gives)
        def _():
            g_a[0].got()
            g_a[1].got()
            wgrad_ref[...] = agot[0].astype(F32) + agot[1].astype(F32)

    def finish(c):
        f_z[c].got()
        b_z[c].got()
        lanes = slice(c * LANES, (c + 1) * LANES)
        proj_ref[:, lanes] = (fpart[c, x, 0].astype(F32) + fzgot[c].astype(F32)).astype(BF16)
        agrad_ref[:, lanes] = (bown[c] + bzgot[c].astype(F32)).astype(BF16)

    weights_a()
    gather_z(0)
    gather_z(1)
    gather_x0()
    weights_line()
    weights_y(0)
    gather_x1(0)
    weights_y(1)
    gather_x1(1)
    weights_core(0)
    weights_core(1)
    gathered(0)
    gathered(1)
    gradient(0)
    gradient(1)
    weights_end()
    forward(0)
    forward(1)
    backward(0)
    b_z[0].start()
    gradient_y(0)
    gradient_y(1)
    forward_sum(0)
    f_z[0].start()
    backward(1)
    forward_sum(1)
    gradient_z(0)
    gradient_z(1)
    b_z[1].start()
    f_z[1].start()
    gradient_sum()
    finish(0)
    finish(1)
    gradient_end()

    for w in wires:
        w.sent()

    assert counter[0] <= N_WIRES


def on_device(attn_out, w_out, cotangent):
    tokens, block = attn_out.shape
    vmem = pl.BlockSpec(memory_space=pltpu.VMEM)
    rows = 2 * BLOCK

    def buf(*shape, dtype=BF16):
        return pltpu.VMEM(shape, dtype)

    proj, agrad, wgrad = pl.pallas_call(
        kernel,
        out_shape=(
            jax.ShapeDtypeStruct((block, tokens), BF16),
            jax.ShapeDtypeStruct((block, tokens), BF16),
            jax.ShapeDtypeStruct((SHARD, BLOCK), F32),
        ),
        in_specs=[pl.BlockSpec(memory_space=pltpu.HBM)] * 3,
        out_specs=(vmem,) * 3,
        scratch_shapes=[
            buf(BLOCK, tokens),
            buf(BLOCK, tokens),
            buf(CHUNKS, 2, BLOCK, LANES),
            buf(CHUNKS, 4, 2, BLOCK, LANES),
            buf(2, 2, 2, 2, 2, SHARD, rows),
            buf(SHARD, BLOCK),
            buf(3, SHARD, BLOCK),
            buf(rows, 4 * rows),
            buf(CHUNKS, 4, 2, BLOCK, LANES),
            buf(CHUNKS, 3, 2, BLOCK, LANES),
            buf(CHUNKS, BLOCK, LANES),
            buf(CHUNKS, BLOCK, LANES),
            buf(CHUNKS, BLOCK, LANES),
            buf(CHUNKS, BLOCK, LANES),
            buf(CHUNKS, BLOCK, LANES, dtype=F32),
            buf(4, 2, 2, 2, SHARD, rows),
            buf(4, 2, 2, SHARD, rows),
            buf(2, 2, 2, 2, SHARD, rows),
            buf(2, 3, 2, SHARD, rows),
            buf(2, 2, SHARD, rows),
            buf(3, 2, SHARD, rows),
            buf(2, SHARD, rows, dtype=F32),
            buf(3, SHARD, BLOCK),
            buf(3, SHARD, BLOCK),
            pltpu.SemaphoreType.DMA((3,)),
            pltpu.SemaphoreType.DMA((N_WIRES,)),
            pltpu.SemaphoreType.DMA((N_WIRES,)),
        ],
        compiler_params=pltpu.CompilerParams(
            collective_id=0, has_side_effects=True, vmem_limit_bytes=VMEM_LIMIT
        ),
    )(attn_out.T, w_out.T, cotangent.T)
    return proj.T, agrad.T, wgrad.T


def solution(mesh):
    return jax.shard_map(
        on_device,
        mesh=mesh,
        in_specs=(P("dp", "mp"), P("mp", "dp"), P("dp", "mp")),
        out_specs=(P("dp", "mp"), P("dp", "mp"), P("mp", "dp")),
        check_vma=False,
    )
```
